128 devices in a mesh: branch: 4 (over z), frame: 16 (over y_hi, x, core), row: 2 (over y_lo).
Axes of the slice: x: 4, y: 4 (y_hi: 2, y_lo: 2; y = y_hi * 2 + y_lo), z: 4, core: 2. Of those that a mesh axis runs over, the one named last changes fastest.
Arguments:
- features: bfloat16 [32, 96, 96, 320], P('frame', 'row'), may hold values from -6 to 6
- offsets: bfloat16 [4, 32, 96, 96, 320], P('branch', 'frame', 'row'), may hold values from -6 to 6
- conv_weight: bfloat16 [4, 3, 3, 320, 320], P('branch'), may hold values from -0.109375 to 0.109375
- conv_bias: float32 [4, 320], P('branch'), may hold values from -3 to 3
- time_weight: bfloat16 [4, 3, 320, 320], P('branch'), may hold values from -0.1875 to 0.1875
- proj_weight: bfloat16 [4, 320, 320], P('branch'), may hold values from -0.3125 to 0.3125
- flags: int32 [3, 32], P(None, 'frame'), may hold values 0 or 1
- scales: int32 [3], replicated, may hold values from 4 to 16
Outputs:
- mixed: bfloat16 [32, 96, 96, 320], P('frame', 'row')
The draws below stay inside these ranges and needn't reach their ends.
All inputs are finite; a program needn't handle non-finite values. No bound on the sum of `flags` on one device may be relied on, other than what follows from the above.
Results may differ from the reference program's by a relative error of at most 0.012.
Values may be sent and summed in bfloat16 or wider, within the bound.
No kernel may reach another device: no remote copies, remote signals or barrier semaphores. Data moves between devices by JAX's collectives and lax.ppermute only.
A program may use at most 320 MiB of HBM per device.

```python
import jax
import jax.numpy as jnp
from jax import lax

C = 320
COLS = 96
CONTROLS = 3
BRANCHES = 4
FRAMES = 32
HEIGHT = 96


def set_ends(array, own_key, smallest, largest):
    longest = array.shape.index(max(array.shape))
    spots = []
    for shift in (0, 1):
        where = [jax.random.randint(jax.random.fold_in(own_key, axis), (), 0, length) for axis, length in enumerate(array.shape)]
        where[longest] = (where[longest] + shift) % array.shape[longest]
        spots.append(tuple(where))
    return array.at[spots[0]].set(smallest).at[spots[1]].set(largest)


def levels(stream_key, extent, pieces, smallest, largest):
    loudness, own = 1.0, jax.random.fold_in(stream_key, 6)
    for dim, parts in pieces:
        heights = jnp.exp(jax.random.uniform(jax.random.fold_in(own, dim), (parts,), jnp.float32, smallest / len(pieces), largest / len(pieces)))
        loudness = loudness * jnp.repeat(heights, extent[dim] // parts).reshape([-1 if axis == dim else 1 for axis in range(len(extent))])
    return loudness


def noise(rng, dims, width, reach, shards=(), held_as=jnp.bfloat16):
    drawn = width * jax.random.normal(rng, dims, jnp.float32)
    if shards:
        drawn = drawn * levels(rng, dims, shards, -0.22, 0.18)
    return jnp.clip(drawn, -reach, reach).astype(held_as)


def setup_inputs(seed: int = 0) -> dict:
    key_of = jax.random.split(jax.random.key(seed), 9)
    return {
        "features": noise(key_of[0], (FRAMES, HEIGHT, COLS, C), 1.0, 6.0, ((0, 16), (1, 2))),
        "offsets": noise(key_of[1], (BRANCHES, FRAMES, HEIGHT, COLS, C), 1.0, 6.0, ((0, 4), (1, 16), (2, 2))),
        "conv_weight": noise(key_of[2], (BRANCHES, 3, 3, C, C), (9 * C) ** -0.5, 0.109375, ((0, 4),)),
        "conv_bias": noise(key_of[3], (BRANCHES, C), 0.5, 3.0, ((0, 4),), jnp.float32),
        "time_weight": noise(key_of[4], (BRANCHES, 3, C, C), (3 * C) ** -0.5, 0.1875, ((0, 4),)),
        "proj_weight": noise(key_of[5], (BRANCHES, C, C), C ** -0.5, 0.3125, ((0, 4),)),
        "flags": set_ends((jax.random.randint(key_of[6], (CONTROLS, FRAMES), 0, 4) < 3).astype(jnp.int32), jax.random.fold_in(key_of[6], 1), 0, 1),
        "scales": jax.random.randint(key_of[7], (CONTROLS,), 4, 17).astype(jnp.int32),
    }


def reference(features, offsets, conv_weight, conv_bias, time_weight, proj_weight, flags, scales):
    total = jnp.zeros(features.shape, jnp.float32)
    for branch in range(CONTROLS + 1):
        inputs = (features.astype(jnp.float32) + offsets[branch].astype(jnp.float32)).astype(jnp.bfloat16)
        conv = lax.conv_general_dilated(inputs.astype(jnp.float32), conv_weight[branch].astype(jnp.float32), (1, 1), "SAME", dimension_numbers=("NHWC", "HWIO", "NHWC"), precision=lax.Precision.HIGHEST)
        spatial = jax.nn.silu(conv + conv_bias[branch]).astype(jnp.bfloat16)
        padded = jnp.pad(spatial, ((1, 1), (0, 0), (0, 0), (0, 0))).astype(jnp.float32)
        acc = inputs.astype(jnp.float32)
        for k in range(3):
            acc = acc + jnp.einsum("fhwc,cd->fhwd", padded[k:k + FRAMES], time_weight[branch, k].astype(jnp.float32), precision=lax.Precision.HIGHEST)
        temporal = acc.astype(jnp.bfloat16)
        proj = jnp.einsum("fhwc,cd->fhwd", temporal.astype(jnp.float32), proj_weight[branch].astype(jnp.float32), precision=lax.Precision.HIGHEST)
        if branch == 0:
            gain = jnp.ones((FRAMES,), jnp.float32)
        else:
            gain = scales[branch - 1].astype(jnp.float32) / 8.0 * flags[branch - 1].astype(jnp.float32)
        term = lax.optimization_barrier((proj * gain[:, None, None, None]).astype(jnp.bfloat16))
        total = total + term.astype(jnp.float32)
    return total.astype(jnp.bfloat16)
```

```python
import functools

import jax
import jax.numpy as jnp
from jax import lax
from jax.experimental import pallas as pl
from jax.experimental.pallas import tpu as pltpu
from jax.sharding import PartitionSpec as P

F32 = jnp.float32
BF16 = jnp.bfloat16
PART = jnp.bfloat16
MAIN = 256
TAIL = 64
LIMIT = 20 * 1024 * 1024
WIDE = 45 * 1024 * 1024
MUCH = 45 * 1024 * 1024


def vmem():
    return pl.BlockSpec(memory_space=pltpu.VMEM)


def smem():
    return pl.BlockSpec(memory_space=pltpu.SMEM)


def hbm():
    return pl.BlockSpec(memory_space=pltpu.HBM)


def token_spec():
    return jax.ShapeDtypeStruct((8, 128), F32)


def move(src, dst, sem):
    copy = pltpu.make_async_copy(src, dst, sem)
    copy.start()
    return copy


def pack_to(ref, start, value):
    size = value.shape[0]
    half = size // 2
    ref[pl.ds(start, size)] = value[:, :128]
    ref[pl.ds(start + size, size)] = value[:, 128:MAIN]
    ref[pl.ds(start + 2 * size, half)] = jnp.concatenate(
        [value[:half, MAIN:], value[half:, MAIN:]], axis=1
    )


def unpack_from(ref, start, size):
    half = size // 2
    tail = ref[pl.ds(start + 2 * size, half)]
    return (
        ref[pl.ds(start, size)],
        ref[pl.ds(start + size, size)],
        jnp.concatenate([tail[:, :TAIL], tail[:, TAIL:]], axis=0),
    )


def edge_kernel(feat_ref, off_ref, out_ref, token_ref, feat, off, sems):
    token_ref[...] = jnp.zeros_like(token_ref)
    frames, rows, width, channels = feat_ref.shape
    row = jnp.where(lax.axis_index("row") == 0, rows - 1, 0)
    copies = []
    for f in range(frames):
        copies.append(move(feat_ref.at[f, row], feat.at[f], sems.at[f, 0]))
        copies.append(move(off_ref.at[0, f, row], off.at[f], sems.at[f, 1]))
    for copy in copies:
        copy.wait()
    x = (feat[...].astype(F32) + off[...].astype(F32)).astype(BF16)
    for f in range(frames):
        pack_to(out_ref, f * width * 5 // 2, x[f])


def edges(features, offsets):
    frames, rows, width, channels = features.shape
    return pl.pallas_call(
        edge_kernel,
        out_shape=[jax.ShapeDtypeStruct((frames * width * 5 // 2, 128), BF16), token_spec()],
        in_specs=[hbm(), hbm()],
        out_specs=[vmem(), vmem()],
        scratch_shapes=[
            pltpu.VMEM((frames, width, channels), BF16),
            pltpu.VMEM((frames, width, channels), BF16),
            pltpu.SemaphoreType.DMA((frames, 2)),
        ],
        name="edges",
    )(features, offsets)


def ring_bits(kind):
    z = lax.axis_index("branch")
    u = jnp.where((z == 1) | (z == 2), 1, 0)
    v = jnp.where(z >= 2, 1, 0)
    return (u, v) if kind == "A" else (v, u)


def ring_pairs(kind):
    first = [(0, 1), (1, 0), (2, 3), (3, 2)]
    second = [(1, 2), (2, 1), (3, 0), (0, 3)]
    return (first, second) if kind == "A" else (second, first)


def weights_kernel(conv_ref, time_ref, proj_ref, main_ref, tail_ref, local_ref, near_ref,
                   conv, time, proj, sems):
    loads = [move(conv_ref.at[0], conv, sems.at[0]), move(time_ref.at[0], time, sems.at[1]),
             move(proj_ref.at[0], proj, sems.at[2])]
    loads[1].wait()
    loads[2].wait()
    last = proj[...]
    channels = last.shape[0]
    both = [jnp.dot(time[k], last, preferred_element_type=F32).astype(BF16) for k in range(3)]
    near_ref[0] = both[0]
    near_ref[1] = both[2]
    for f, blocks in enumerate(((last, both[1], both[2]), (last, both[0], both[1]))):
        for k, w in enumerate(blocks):
            local_ref[f, k * MAIN : (k + 1) * MAIN] = w[:MAIN]
            local_ref[f, 3 * MAIN + k * TAIL : 3 * MAIN + (k + 1) * TAIL] = w[MAIN:]
        local_ref[f, 3 * MAIN + 3 * TAIL :] = jnp.zeros((TAIL, channels), BF16)
    zero = jnp.zeros((TAIL, MAIN), BF16)
    loads[0].wait()
    for p in range(3):
        for q in range(3):
            w = conv[p, q]
            main_ref[p, q * MAIN : (q + 1) * MAIN] = w[:MAIN, :MAIN]
            main_ref[p, 3 * MAIN + q * TAIL : 3 * MAIN + (q + 1) * TAIL] = w[MAIN:, :MAIN]
        main_ref[p, 3 * MAIN + 3 * TAIL :] = zero
    for q in range(3):
        w = jnp.concatenate(
            [conv[p, q][:, MAIN:] for p in range(3)] + [jnp.zeros((MAIN + TAIL, TAIL), BF16)],
            axis=1,
        )
        tail_ref[q * MAIN : (q + 1) * MAIN] = w[:MAIN]
        tail_ref[3 * MAIN + q * TAIL : 3 * MAIN + (q + 1) * TAIL] = w[MAIN:]
    tail_ref[3 * MAIN + 3 * TAIL :] = zero


def sums_kernel(windows, with_weights, feat_ref, off_ref, *refs):
    count = len(windows)
    frames, rows, width, channels = feat_ref.shape
    if with_weights:
        conv_ref, time_ref, proj_ref, _, *refs = refs
    else:
        _, *refs = refs
    x_refs, refs = refs[:count], refs[count:]
    if with_weights:
        made, refs = refs[:4], refs[4:]
    token_ref, feat, off, sems, *refs = refs
    token_ref[...] = jnp.zeros_like(token_ref)
    copies = []
    for i, (low, high) in enumerate(windows):
        span = high - low
        for f in range(frames):
            window, place = pl.ds(low, span), pl.ds(sum(h - l for l, h in windows[:i]), span)
            copies.append((
                x_refs[i].at[f], f, place,
                move(feat_ref.at[f, window], feat.at[f, place], sems.at[i, f, 0]),
                move(off_ref.at[0, f, window], off.at[f, place], sems.at[i, f, 1]),
            ))
    if with_weights:
        weights_kernel(conv_ref, time_ref, proj_ref, *made, *refs)
    for x_ref, f, place, one, two in copies:
        one.wait()
        two.wait()
        x_ref[...] = feat[f, place] + off[f, place]


def sums(windows, features, offsets, weights, token):
    frames, rows, width, channels = features.shape
    total = sum(high - low for low, high in windows)
    out = [jax.ShapeDtypeStruct((frames, high - low, width, channels), BF16) for low, high in windows]
    scratch = [
        pltpu.VMEM((frames, total, width, channels), BF16),
        pltpu.VMEM((frames, total, width, channels), BF16),
        pltpu.SemaphoreType.DMA((len(windows), frames, 2)),
    ]
    if weights:
        out += [
            jax.ShapeDtypeStruct((3, 4 * MAIN, MAIN), BF16),
            jax.ShapeDtypeStruct((4 * MAIN, MAIN), BF16),
            jax.ShapeDtypeStruct((2, 4 * MAIN, channels), BF16),
            jax.ShapeDtypeStruct((2, channels, channels), BF16),
        ]
        scratch += [pltpu.VMEM(w.shape[1:], BF16) for w in weights]
        scratch += [pltpu.SemaphoreType.DMA((3,))]
    out.append(token_spec())
    return pl.pallas_call(
        functools.partial(sums_kernel, tuple(windows), bool(weights)),
        out_shape=out,
        in_specs=[hbm()] * (2 + len(weights)) + [vmem()],
        out_specs=[vmem()] * len(out),
        scratch_shapes=scratch,
        compiler_params=pltpu.CompilerParams(vmem_limit_bytes=WIDE if weights else MUCH),
        name="sums_weights" if weights else "sums",
    )(features, offsets, *weights, token)


def silu(v):
    half = 0.5 * v
    return half + half * jnp.tanh(half)


def conv_kernel(first, count, rows, x_ref, halo_ref, main_ref, tail_ref, local_ref, bias_ref, _, *rest):
    near_ref, far_ref, part_ref, token_ref, cols3, cols4, outs = rest
    token_ref[...] = jnp.zeros_like(token_ref)
    frames, _, width, channels = x_ref.shape
    begin = first - max(first - 1, 0)
    span, size = count + 2, count * width
    side = lax.axis_index("row")
    bias = bias_ref[...]
    column = lax.broadcasted_iota(jnp.int32, (span, width, 1), 1)
    for f in range(frames):
        x = x_ref[f].astype(F32)
        for here, at, outside in ((first == 0, 0, 0), (first + count == rows, 1, 1)):
            if here:
                pieces = unpack_from(halo_ref, f * width * 5 // 2, width)
                edge = jnp.concatenate(pieces, axis=1).astype(F32)
                edge = (edge * jnp.where(side == outside, 0.0, 1.0))[None]
                x = jnp.concatenate([edge, x] if at == 0 else [x, edge], axis=0)
        flat = x.reshape(span * width, channels)
        before = pltpu.roll(flat, 1, 0).reshape(x.shape)
        after = pltpu.roll(flat, span * width - 1, 0).reshape(x.shape)
        before = jnp.where(column == 0, 0.0, before).reshape(flat.shape)
        after = jnp.where(column == width - 1, 0.0, after).reshape(flat.shape)
        parts = [v.astype(BF16) for v in (before, flat, after)]
        for q in range(3):
            cols3[f, :, q * MAIN : (q + 1) * MAIN] = parts[q][:, :MAIN]
        cols3[f, :, 3 * MAIN :] = jnp.concatenate(
            [v[:, MAIN:] for v in parts] + [jnp.zeros((span * width, TAIL), BF16)], axis=1
        )
        acc = bias[:, :MAIN]
        for p in range(3):
            acc = acc + jnp.dot(
                cols3[f, p * width : p * width + size], main_ref[p], preferred_element_type=F32
            )
        main = silu(acc).astype(BF16)
        three = jnp.dot(cols3[f], tail_ref[...], preferred_element_type=F32)
        acc = bias[:, MAIN:]
        for p in range(3):
            acc = acc + three[p * width : p * width + size, p * TAIL : (p + 1) * TAIL]
        tail = silu(acc).astype(BF16)
        outs[f, :size] = main[:, :128]
        outs[f, size : 2 * size] = main[:, 128:]
        outs[f, 2 * size :] = jnp.concatenate([tail[: size // 2], tail[size // 2 :]], axis=1)
        for g in range(frames):
            cols4[g, :, (f + 1) * MAIN : (f + 2) * MAIN] = main
        cols4[f, :, :MAIN] = parts[1][width : width + size, :MAIN]
    for f in range(frames):
        tails = [x_ref[f, begin : begin + count].reshape(size, channels)[:, MAIN:]]
        tails += [unpack_from(outs.at[g], 0, size)[2] for g in range(frames)]
        tails.append(jnp.zeros((size, TAIL), BF16))
        cols4[f, :, 3 * MAIN :] = jnp.concatenate(tails, axis=1)
        total = jnp.dot(cols4[f], local_ref[f], preferred_element_type=F32)
        pack_to(part_ref, f * size * 5 // 2, total.astype(PART))
    odd = lax.rem(lax.axis_index("frame"), 2)
    near_ref[...] = outs[1 - odd]
    far_ref[...] = outs[odd]


def conv_rows(first, count, rows, x, halo, weights, bias, token):
    frames, _, width, channels = x.shape
    span, size = count + 2, count * width
    own = jax.ShapeDtypeStruct((size * 5 // 2, 128), BF16)
    return pl.pallas_call(
        functools.partial(conv_kernel, first, count, rows),
        out_shape=[own, own, jax.ShapeDtypeStruct((frames * size * 5 // 2, 128), PART), token_spec()],
        in_specs=[vmem()] * 7,
        out_specs=[vmem()] * 4,
        scratch_shapes=[
            pltpu.VMEM((frames, span * width, 4 * MAIN), BF16),
            pltpu.VMEM((frames, size, 4 * MAIN), BF16),
            pltpu.VMEM((frames, size * 5 // 2, 128), BF16),
        ],
        compiler_params=pltpu.CompilerParams(vmem_limit_bytes=LIMIT),
        cost_estimate=pl.CostEstimate(
            flops=2 * frames * size * 12 * channels * channels,
            bytes_accessed=6 * frames * size * channels,
            transcendentals=frames * size * channels,
        ),
        name=f"conv_{first}",
    )(x, halo, *weights[:3], bias, token)


def term_kernel(kind, inside_ref, across_ref, part_ref, near_ref, flag_ref, scale_ref, _, *rest):
    *out_refs, token_ref, packed = rest
    token_ref[...] = jnp.zeros_like(token_ref)
    size = inside_ref.shape[0] * 2 // 5
    odd = lax.rem(lax.axis_index("frame"), 2)
    branch = lax.axis_index("branch")
    control = jnp.maximum(branch - 1, 0)
    target = out_refs[0] if kind == "S" else packed
    for f, ref in ((1 - odd, inside_ref), (odd, across_ref)):
        base = f * (size * 5 // 2)
        value = jnp.concatenate(unpack_from(ref, 0, size), axis=1)
        term = jnp.dot(value, near_ref[f], preferred_element_type=F32)
        gain = scale_ref[control].astype(F32) / 8.0 * flag_ref[control, f].astype(F32)
        gain = jnp.where(branch == 0, 1.0, gain)
        pieces = [
            term[:, :128],
            term[:, 128:MAIN],
            jnp.concatenate([term[: size // 2, MAIN:], term[size // 2 :, MAIN:]], axis=1),
        ]
        for piece, start in zip(pieces, (base, base + size, base + 2 * size)):
            where = pl.ds(pl.multiple_of(start, 16), piece.shape[0])
            target[where] = ((piece + part_ref[where].astype(F32)) * gain).astype(BF16)
    if kind != "S":
        near_bit, _ = ring_bits(kind)
        half = packed.shape[0] // 2
        for ref, which in zip(out_refs, (1 - near_bit, near_bit)):
            ref[...] = packed[pl.ds(pl.multiple_of(which * half, 16), half)]


def terms(name, kind, prev, after, part, near, flags, scales, token):
    total = part.shape[0]
    parts = 1 if kind == "S" else 2
    return pl.pallas_call(
        functools.partial(term_kernel, kind),
        out_shape=[jax.ShapeDtypeStruct((total // parts, 128), BF16)] * parts + [token_spec()],
        in_specs=[vmem()] * 4 + [smem()] * 2 + [vmem()],
        out_specs=[vmem()] * (parts + 1),
        scratch_shapes=[pltpu.VMEM((total, 128), BF16)],
        compiler_params=pltpu.CompilerParams(vmem_limit_bytes=LIMIT),
        cost_estimate=pl.CostEstimate(
            flops=2 * total * 128 * 320, bytes_accessed=10 * total * 128, transcendentals=0
        ),
        name=f"terms_{name}",
    )(prev, after, part, near, flags, scales, token)


def add_kernel(kind, keep_ref, got_ref, _, send_ref, next_ref, token_ref):
    token_ref[...] = jnp.zeros_like(token_ref)
    _, far = ring_bits(kind)
    half = keep_ref.shape[0] // 2
    for ref, which in zip((send_ref, next_ref), (1 - far, far)):
        part = pl.ds(pl.multiple_of(which * half, 16), half)
        ref[...] = (keep_ref[part].astype(F32) + got_ref[part].astype(F32)).astype(BF16)


def add_last_kernel(keep_ref, got_ref, _, sum_ref, token_ref):
    token_ref[...] = jnp.zeros_like(token_ref)
    sum_ref[...] = (keep_ref[...].astype(F32) + got_ref[...].astype(F32)).astype(BF16)


def join_kernel(mine_ref, other_ref, _, both_ref, token_ref):
    token_ref[...] = jnp.zeros_like(token_ref)
    size = mine_ref.shape[0]
    both_ref[:size] = mine_ref[...]
    both_ref[size:] = other_ref[...]


def small(name, kernel, shapes, *operands):
    return pl.pallas_call(
        kernel,
        out_shape=[jax.ShapeDtypeStruct((rows, 128), BF16) for rows in shapes] + [token_spec()],
        in_specs=[vmem()] * len(operands),
        out_specs=[vmem()] * (len(shapes) + 1),
        compiler_params=pltpu.CompilerParams(vmem_limit_bytes=LIMIT),
        cost_estimate=pl.CostEstimate(
            flops=shapes[0] * 128, bytes_accessed=6 * shapes[0] * 128, transcendentals=0
        ),
        name=name,
    )(*operands)


def unpack_kernel(first, count, kind, grown, *refs):
    if grown:
        refs = refs[1:]
    if kind == "S":
        packed, _, out_ref, token_ref, held, sems = refs
    else:
        mine, other, across, _, out_ref, token_ref, packed, held, sems = refs
        near, far = ring_bits(kind)
        part = mine.shape[0]
        for ref, where in (
            (mine, near * 2 + far),
            (other, near * 2 + 1 - far),
            (across.at[pl.ds(0, part)], (1 - near) * 2 + far),
            (across.at[pl.ds(part, part)], (1 - near) * 2 + 1 - far),
        ):
            packed[pl.ds(pl.multiple_of(where * part, 16), part)] = ref[...]
    token_ref[...] = jnp.zeros_like(token_ref)
    frames, _, width, channels = held.shape
    size = count * width
    copies = []
    for f in range(frames):
        base = (5 * f) * (size // 2)
        shape = (count, width, 128)
        held[f, :, :, :128] = packed[base : base + size].reshape(shape)
        held[f, :, :, 128:256] = packed[base + size : base + 2 * size].reshape(shape)
        tails = packed[base + 2 * size : base + 2 * size + size // 2].reshape(count // 2, width, 128)
        held[f, : count // 2, :, MAIN:] = tails[:, :, :TAIL]
        held[f, count // 2 :, :, MAIN:] = tails[:, :, TAIL:]
        copies.append(move(held.at[f], out_ref.at[f, pl.ds(first, count)], sems.at[f]))
    for copy in copies:
        copy.wait()


def unpack(first, count, kind, shape, parts, token, grown):
    frames, _, width, channels = shape
    old = [] if grown is None else [grown]
    scratch = [
        pltpu.VMEM((frames, count, width, channels), BF16),
        pltpu.SemaphoreType.DMA((frames,)),
    ]
    if kind != "S":
        scratch.insert(0, pltpu.VMEM((frames * count * width * 5 // 2, 128), BF16))
    return pl.pallas_call(
        functools.partial(unpack_kernel, first, count, kind, grown is not None),
        out_shape=[jax.ShapeDtypeStruct(shape, BF16), token_spec()],
        in_specs=[hbm()] * len(old) + [vmem()] * (len(parts) + 1),
        out_specs=[hbm(), vmem()],
        scratch_shapes=scratch,
        input_output_aliases={0: 0} if old else {},
        compiler_params=pltpu.CompilerParams(vmem_limit_bytes=LIMIT),
        cost_estimate=pl.CostEstimate(
            flops=0, bytes_accessed=4 * frames * count * width * channels, transcendentals=0
        ),
        name=f"unpack_{first}",
    )(*old, *parts, token)


def plan(rows):
    if rows == 48:
        return [(8, 8, "A"), (16, 12, "B"), (28, 12, "A"), (0, 8, "B"), (40, 8, "A")]
    size = rows // 6
    kinds = "ABABAB"
    return [(size * i, size, kinds[i]) for i in (1, 2, 3, 4, 0, 5)]


def order(count):
    if count == 5:
        return [
            ("C", 0), ("T", 0), ("C", 1), ("A", 0), ("C", 2), ("L", 0),
            ("T", 1), ("C", 3), ("J", 0), ("T", 2), ("T", 3), ("A", 1),
            ("C", 4), ("A", 3), ("U", 0), ("T", 4), ("A", 2), ("L", 1),
            ("L", 2), ("L", 3), ("J", 2), ("A", 4), ("L", 4), ("J", 1),
            ("J", 3), ("J", 4), ("U", 2), ("U", 1), ("U", 4), ("U", 3),
        ]
    lags = {"C": 0, "T": 1, "A": 2, "L": 3, "J": 4, "U": 5}
    steps = []
    for slot in range(count + 6):
        for step in "CTALJU":
            chunk = slot - lags[step]
            if 0 <= chunk < count:
                steps.append((step, chunk))
    return steps


def on_device(features, offsets, conv_weight, conv_bias, time_weight, proj_weight, flags, scales):
    rows = features.shape[1]
    edge, token = edges(features, offsets)
    halo = lax.ppermute(edge, "row", [(0, 1), (1, 0)])
    chunks = plan(rows)
    windows = [(max(first - 1, 0), min(first + size + 1, rows)) for first, size, _ in chunks]
    given = (conv_weight, time_weight, proj_weight)
    x, *weights, token = sums(windows[:1], features, offsets, given, token)
    near = weights[3]
    xs = [x]
    count = lax.axis_size("frame")
    inside = [(i, i ^ 1) for i in range(count)]
    across = [(i, j) for i in range(1, count - 1, 2) for j in (i + 1,)]
    across += [(j, i) for i, j in across]
    blank = jnp.zeros_like(halo)
    live = [{} for _ in chunks]
    out = None
    for step, i in order(len(chunks)):
        first, size, kind = chunks[i]
        pairs = ring_pairs(kind)
        now = live[i]
        if step == "C":
            edge = halo if first == 0 or first + size == rows else blank
            near_edge, far_edge, now["part"], token = conv_rows(
                first, size, rows, xs[i], edge, weights, conv_bias, token
            )
            now["prev"] = lax.ppermute(far_edge, "frame", across)
            now["next"] = lax.ppermute(near_edge, "frame", inside)
            if i == 0:
                *more, token = sums(windows[1:], features, offsets, (), token)
                xs += more
        elif step == "T":
            send, now["keep"], token = terms(
                first, kind, now["next"], now["prev"], now["part"], near, flags, scales, token
            )
            now["got"] = lax.ppermute(send, "branch", pairs[0])
        elif step == "A":
            half = now["keep"].shape[0] // 2
            send, now["keep"], token = small(
                f"add_{first}", functools.partial(add_kernel, kind), (half, half),
                now["keep"], now["got"], token,
            )
            now["got"] = lax.ppermute(send, "branch", pairs[1])
        elif step == "L":
            now["mine"], token = small(
                f"last_{first}", add_last_kernel, now["keep"].shape[:1], now["keep"], now["got"], token
            )
            now["other"] = lax.ppermute(now["mine"], "branch", pairs[1])
        elif step == "J":
            both, token = small(
                f"join_{first}", join_kernel, (2 * now["mine"].shape[0],),
                now["mine"], now["other"], token,
            )
            now["across"] = lax.ppermute(both, "branch", pairs[0])
        else:
            parts = (now["mine"], now["other"], now["across"])
            out, token = unpack(first, size, kind, features.shape, parts, token, out)
    return out


def solution(mesh):
    return jax.shard_map(
        on_device,
        mesh=mesh,
        in_specs=(
            P("frame", "row", None, None),
            P("branch", "frame", "row", None, None),
            P("branch", None, None, None, None),
            P("branch", None),
            P("branch", None, None, None),
            P("branch", None, None),
            P(None, "frame"),
            P(),
        ),
        out_specs=P("frame", "row", None, None),
        check_vma=False,
    )
```

```python
import functools

import jax
import jax.numpy as jnp
from jax import lax
from jax.experimental import pallas as pl
from jax.experimental.pallas import tpu as pltpu
from jax.sharding import PartitionSpec as P

F32 = jnp.float32
BF16 = jnp.bfloat16
PART = jnp.bfloat16
SCALE = 1.0
MAIN = 256
TAIL = 64
LIMIT = 20 * 1024 * 1024
WIDE = 45 * 1024 * 1024
MUCH = 45 * 1024 * 1024
CONV = 20 * 1024 * 1024


def vmem():
    return pl.BlockSpec(memory_space=pltpu.VMEM)


def smem():
    return pl.BlockSpec(memory_space=pltpu.SMEM)


def hbm():
    return pl.BlockSpec(memory_space=pltpu.HBM)


def token_spec():
    return jax.ShapeDtypeStruct((8, 128), F32)


def move(src, dst, sem):
    copy = pltpu.make_async_copy(src, dst, sem)
    copy.start()
    return copy


def pack_to(ref, start, value):
    size = value.shape[0]
    half = size // 2
    ref[pl.ds(start, size)] = value[:, :128]
    ref[pl.ds(start + size, size)] = value[:, 128:MAIN]
    ref[pl.ds(start + 2 * size, half)] = jnp.concatenate(
        [value[:half, MAIN:], value[half:, MAIN:]], axis=1
    )


def unpack_from(ref, start, size):
    half = size // 2
    tail = ref[pl.ds(start + 2 * size, half)]
    return (
        ref[pl.ds(start, size)],
        ref[pl.ds(start + size, size)],
        jnp.concatenate([tail[:, :TAIL], tail[:, TAIL:]], axis=0),
    )


def edge_kernel(feat_ref, off_ref, out_ref, token_ref, feat, off, sems):
    token_ref[...] = jnp.zeros_like(token_ref)
    frames, rows, width, channels = feat_ref.shape
    row = jnp.where(lax.axis_index("row") == 0, rows - 1, 0)
    copies = []
    for f in range(frames):
        copies.append(move(feat_ref.at[f, row], feat.at[f], sems.at[f, 0]))
        copies.append(move(off_ref.at[0, f, row], off.at[f], sems.at[f, 1]))
    for copy in copies:
        copy.wait()
    x = (feat[...].astype(F32) + off[...].astype(F32)).astype(BF16)
    for f in range(frames):
        pack_to(out_ref, f * width * 5 // 2, x[f])


def edges(features, offsets):
    frames, rows, width, channels = features.shape
    return pl.pallas_call(
        edge_kernel,
        out_shape=[jax.ShapeDtypeStruct((frames * width * 5 // 2, 128), BF16), token_spec()],
        in_specs=[hbm(), hbm()],
        out_specs=[vmem(), vmem()],
        scratch_shapes=[
            pltpu.VMEM((frames, width, channels), BF16),
            pltpu.VMEM((frames, width, channels), BF16),
            pltpu.SemaphoreType.DMA((frames, 2)),
        ],
        name="edges",
    )(features, offsets)


def ring_bits(kind):
    z = lax.axis_index("branch")
    u = jnp.where((z == 1) | (z == 2), 1, 0)
    v = jnp.where(z >= 2, 1, 0)
    return (u, v) if kind == "A" else (v, u)


def ring_pairs(kind):
    first = [(0, 1), (1, 0), (2, 3), (3, 2)]
    second = [(1, 2), (2, 1), (3, 0), (0, 3)]
    return (first, second) if kind == "A" else (second, first)


def weights_kernel(conv_ref, time_ref, proj_ref, main_ref, tail_ref, local_ref, near_ref,
                   conv, time, proj, sems):
    loads = [move(conv_ref.at[0], conv, sems.at[0]), move(time_ref.at[0], time, sems.at[1]),
             move(proj_ref.at[0], proj, sems.at[2])]
    loads[1].wait()
    loads[2].wait()
    last = proj[...]
    channels = last.shape[0]
    both = [jnp.dot(time[k], last, preferred_element_type=F32).astype(BF16) for k in range(3)]
    near_ref[0] = both[0]
    near_ref[1] = both[2]
    for f, blocks in enumerate(((last, both[1], both[2]), (last, both[0], both[1]))):
        for k, w in enumerate(blocks):
            local_ref[f, k * MAIN : (k + 1) * MAIN] = w[:MAIN]
            local_ref[f, 3 * MAIN + k * TAIL : 3 * MAIN + (k + 1) * TAIL] = w[MAIN:]
        local_ref[f, 3 * MAIN + 3 * TAIL :] = jnp.zeros((TAIL, channels), BF16)
    zero = jnp.zeros((TAIL, MAIN), BF16)
    loads[0].wait()
    for p in range(3):
        for q in range(3):
            w = conv[p, q]
            main_ref[p, q * MAIN : (q + 1) * MAIN] = w[:MAIN, :MAIN]
            main_ref[p, 3 * MAIN + q * TAIL : 3 * MAIN + (q + 1) * TAIL] = w[MAIN:, :MAIN]
        main_ref[p, 3 * MAIN + 3 * TAIL :] = zero
    for q in range(3):
        w = jnp.concatenate(
            [conv[p, q][:, MAIN:] for p in range(3)] + [jnp.zeros((MAIN + TAIL, TAIL), BF16)],
            axis=1,
        )
        tail_ref[q * MAIN : (q + 1) * MAIN] = w[:MAIN]
        tail_ref[3 * MAIN + q * TAIL : 3 * MAIN + (q + 1) * TAIL] = w[MAIN:]
    tail_ref[3 * MAIN + 3 * TAIL :] = zero


def sums_kernel(windows, with_weights, feat_ref, off_ref, *refs):
    count = len(windows)
    frames, rows, width, channels = feat_ref.shape
    if not with_weights:
        _, *refs = refs
    if with_weights:
        conv_ref, time_ref, proj_ref, _, *refs = refs
    else:
        _, *refs = refs
    x_refs, refs = refs[:count], refs[count:]
    if with_weights:
        made, refs = refs[:4], refs[4:]
    token_ref, feat, off, sems, *refs = refs
    token_ref[...] = jnp.zeros_like(token_ref)
    copies = []
    for i, (low, high) in enumerate(windows):
        span = high - low
        for f in range(frames):
            window, place = pl.ds(low, span), pl.ds(sum(h - l for l, h in windows[:i]), span)
            copies.append((
                x_refs[i].at[f], f, place,
                move(feat_ref.at[f, window], feat.at[f, place], sems.at[i, f, 0]),
                move(off_ref.at[0, f, window], off.at[f, place], sems.at[i, f, 1]),
            ))
    if with_weights:
        weights_kernel(conv_ref, time_ref, proj_ref, *made, *refs)
    for x_ref, f, place, one, two in copies:
        one.wait()
        two.wait()
        x_ref[...] = feat[f, place] + off[f, place]


def sums(windows, features, offsets, weights, token, early=()):
    frames, rows, width, channels = features.shape
    total = sum(high - low for low, high in windows)
    out = [jax.ShapeDtypeStruct((frames, high - low, width, channels), BF16) for low, high in windows]
    scratch = [
        pltpu.VMEM((frames, total, width, channels), BF16),
        pltpu.VMEM((frames, total, width, channels), BF16),
        pltpu.SemaphoreType.DMA((len(windows), frames, 2)),
    ]
    if weights:
        out += [
            jax.ShapeDtypeStruct((3, 4 * MAIN, MAIN), BF16),
            jax.ShapeDtypeStruct((4 * MAIN, MAIN), BF16),
            jax.ShapeDtypeStruct((2, 4 * MAIN, channels), BF16),
            jax.ShapeDtypeStruct((2, channels, channels), BF16),
        ]
        scratch += [pltpu.VMEM(w.shape[1:], BF16) for w in weights]
        scratch += [pltpu.SemaphoreType.DMA((3,))]
    out.append(token_spec())
    return pl.pallas_call(
        functools.partial(sums_kernel, tuple(windows), bool(weights)),
        out_shape=out,
        in_specs=[hbm()] * (2 + len(weights)) + [vmem()] * (1 + len(early)),
        out_specs=[vmem()] * len(out),
        scratch_shapes=scratch,
        compiler_params=pltpu.CompilerParams(vmem_limit_bytes=WIDE if weights else MUCH),
        name="sums_weights" if weights else "sums",
    )(features, offsets, *weights, *early, token)


def silu(v):
    half = 0.5 * v
    return half + half * jnp.tanh(half)


def conv_kernel(first, count, rows, x_ref, halo_ref, main_ref, tail_ref, local_ref, bias_ref, _, *rest):
    *prior, near_ref, far_ref, part_ref, token_ref, cols3, cols4, outs = rest
    token_ref[...] = jnp.zeros_like(token_ref)
    frames, _, width, channels = x_ref.shape
    begin = first - max(first - 1, 0)
    span, size = count + 2, count * width
    side = lax.axis_index("row")
    bias = bias_ref[...]
    column = lax.broadcasted_iota(jnp.int32, (span, width, 1), 1)
    for f in range(frames):
        x = x_ref[f].astype(F32)
        for here, at, outside in ((first == 0, 0, 0), (first + count == rows, 1, 1)):
            if here:
                pieces = unpack_from(halo_ref, f * width * 5 // 2, width)
                edge = jnp.concatenate(pieces, axis=1).astype(F32)
                edge = (edge * jnp.where(side == outside, 0.0, 1.0))[None]
                x = jnp.concatenate([edge, x] if at == 0 else [x, edge], axis=0)
        flat = x.reshape(span * width, channels)
        before = pltpu.roll(flat, 1, 0).reshape(x.shape)
        after = pltpu.roll(flat, span * width - 1, 0).reshape(x.shape)
        before = jnp.where(column == 0, 0.0, before).reshape(flat.shape)
        after = jnp.where(column == width - 1, 0.0, after).reshape(flat.shape)
        parts = [v.astype(BF16) for v in (before, flat, after)]
        for q in range(3):
            cols3[f, :, q * MAIN : (q + 1) * MAIN] = parts[q][:, :MAIN]
        cols3[f, :, 3 * MAIN :] = jnp.concatenate(
            [v[:, MAIN:] for v in parts] + [jnp.zeros((span * width, TAIL), BF16)], axis=1
        )
        acc = bias[:, :MAIN]
        for p in range(3):
            acc = acc + jnp.dot(
                cols3[f, p * width : p * width + size], main_ref[p], preferred_element_type=F32
            )
        main = silu(acc).astype(BF16)
        three = jnp.dot(cols3[f], tail_ref[...], preferred_element_type=F32)
        acc = bias[:, MAIN:]
        for p in range(3):
            acc = acc + three[p * width : p * width + size, p * TAIL : (p + 1) * TAIL]
        tail = silu(acc).astype(BF16)
        outs[f, :size] = main[:, :128]
        outs[f, size : 2 * size] = main[:, 128:]
        outs[f, 2 * size :] = jnp.concatenate([tail[: size // 2], tail[size // 2 :]], axis=1)
        for g in range(frames):
            cols4[g, :, (f + 1) * MAIN : (f + 2) * MAIN] = main
        cols4[f, :, :MAIN] = parts[1][width : width + size, :MAIN]
    for f in range(frames):
        tails = [x_ref[f, begin : begin + count].reshape(size, channels)[:, MAIN:]]
        tails += [unpack_from(outs.at[g], 0, size)[2] for g in range(frames)]
        tails.append(jnp.zeros((size, TAIL), BF16))
        cols4[f, :, 3 * MAIN :] = jnp.concatenate(tails, axis=1)
        total = jnp.dot(cols4[f], local_ref[f], preferred_element_type=F32)
        pack_to(part_ref, f * size * 5 // 2, total.astype(PART))
    odd = lax.rem(lax.axis_index("frame"), 2)
    for ref, which, old in zip((near_ref, far_ref), (1 - odd, odd), prior or (None, None)):
        held = 0 if old is None else old.shape[0]
        if held:
            ref[:held] = old[...]
        ref[held:] = outs[which]


def conv_rows(first, count, rows, x, halo, weights, bias, token, prior):
    frames, _, width, channels = x.shape
    span, size = count + 2, count * width
    held = prior[0].shape[0] if prior else 0
    own = jax.ShapeDtypeStruct((held + size * 5 // 2, 128), BF16)
    return pl.pallas_call(
        functools.partial(conv_kernel, first, count, rows),
        out_shape=[own, own, jax.ShapeDtypeStruct((frames * size * 5 // 2, 128), PART), token_spec()],
        in_specs=[vmem()] * (7 + len(prior)),
        out_specs=[vmem()] * 4,
        scratch_shapes=[
            pltpu.VMEM((frames, span * width, 4 * MAIN), BF16),
            pltpu.VMEM((frames, size, 4 * MAIN), BF16),
            pltpu.VMEM((frames, size * 5 // 2, 128), BF16),
        ],
        compiler_params=pltpu.CompilerParams(vmem_limit_bytes=CONV),
        cost_estimate=pl.CostEstimate(
            flops=int(SCALE * (2 * frames * size * 12 * channels * channels)),
            bytes_accessed=int(SCALE * (6 * frames * size * channels)),
            transcendentals=int(SCALE * (frames * size * channels)),
        ),
        name=f"conv_{first}",
    )(x, halo, *weights[:3], bias, token, *prior)


def term_kernel(kind, begin, inside_ref, across_ref, part_ref, near_ref, flag_ref, scale_ref, _, *rest):
    *out_refs, token_ref, packed = rest
    token_ref[...] = jnp.zeros_like(token_ref)
    size = part_ref.shape[0] // 5
    odd = lax.rem(lax.axis_index("frame"), 2)
    branch = lax.axis_index("branch")
    control = jnp.maximum(branch - 1, 0)
    target = out_refs[0] if kind == "S" else packed
    for f, ref in ((1 - odd, inside_ref), (odd, across_ref)):
        base = f * (size * 5 // 2)
        value = jnp.concatenate(unpack_from(ref, begin, size), axis=1)
        term = jnp.dot(value, near_ref[f], preferred_element_type=F32)
        gain = scale_ref[control].astype(F32) / 8.0 * flag_ref[control, f].astype(F32)
        gain = jnp.where(branch == 0, 1.0, gain)
        pieces = [
            term[:, :128],
            term[:, 128:MAIN],
            jnp.concatenate([term[: size // 2, MAIN:], term[size // 2 :, MAIN:]], axis=1),
        ]
        for piece, start in zip(pieces, (base, base + size, base + 2 * size)):
            where = pl.ds(pl.multiple_of(start, 16), piece.shape[0])
            target[where] = ((piece + part_ref[where].astype(F32)) * gain).astype(BF16)
    if kind != "S":
        near_bit, _ = ring_bits(kind)
        half = packed.shape[0] // 2
        for ref, which in zip(out_refs, (1 - near_bit, near_bit)):
            ref[...] = packed[pl.ds(pl.multiple_of(which * half, 16), half)]


def terms(name, kind, begin, prev, after, part, near, flags, scales, token):
    total = part.shape[0]
    parts = 1 if kind == "S" else 2
    return pl.pallas_call(
        functools.partial(term_kernel, kind, begin),
        out_shape=[jax.ShapeDtypeStruct((total // parts, 128), BF16)] * parts + [token_spec()],
        in_specs=[vmem()] * 4 + [smem()] * 2 + [vmem()],
        out_specs=[vmem()] * (parts + 1),
        scratch_shapes=[pltpu.VMEM((total, 128), BF16)],
        compiler_params=pltpu.CompilerParams(vmem_limit_bytes=LIMIT),
        cost_estimate=pl.CostEstimate(
            flops=int(SCALE * (2 * total * 128 * 320)), bytes_accessed=int(SCALE * (10 * total * 128)), transcendentals=0
        ),
        name=f"terms_{name}",
    )(prev, after, part, near, flags, scales, token)


def add_kernel(kind, keep_ref, got_ref, _, send_ref, next_ref, token_ref):
    token_ref[...] = jnp.zeros_like(token_ref)
    _, far = ring_bits(kind)
    half = keep_ref.shape[0] // 2
    for ref, which in zip((send_ref, next_ref), (1 - far, far)):
        part = pl.ds(pl.multiple_of(which * half, 16), half)
        ref[...] = (keep_ref[part].astype(F32) + got_ref[part].astype(F32)).astype(BF16)


def add_last_kernel(keep_ref, got_ref, _, sum_ref, token_ref):
    token_ref[...] = jnp.zeros_like(token_ref)
    sum_ref[...] = (keep_ref[...].astype(F32) + got_ref[...].astype(F32)).astype(BF16)


def join_kernel(mine_ref, other_ref, _, both_ref, token_ref):
    token_ref[...] = jnp.zeros_like(token_ref)
    size = mine_ref.shape[0]
    both_ref[:size] = mine_ref[...]
    both_ref[size:] = other_ref[...]


def small(name, kernel, shapes, *operands):
    return pl.pallas_call(
        kernel,
        out_shape=[jax.ShapeDtypeStruct((rows, 128), BF16) for rows in shapes] + [token_spec()],
        in_specs=[vmem()] * len(operands),
        out_specs=[vmem()] * (len(shapes) + 1),
        compiler_params=pltpu.CompilerParams(vmem_limit_bytes=LIMIT),
        cost_estimate=pl.CostEstimate(
            flops=int(SCALE * (shapes[0] * 128)), bytes_accessed=int(SCALE * (6 * shapes[0] * 128)), transcendentals=0
        ),
        name=name,
    )(*operands)


def unpack_kernel(first, count, kind, grown, *refs):
    if grown:
        refs = refs[1:]
    if kind == "S":
        packed, _, out_ref, token_ref, held, sems = refs
    else:
        mine, other, across, _, out_ref, token_ref, packed, held, sems = refs
        near, far = ring_bits(kind)
        part = mine.shape[0]
        for ref, where in (
            (mine, near * 2 + far),
            (other, near * 2 + 1 - far),
            (across.at[pl.ds(0, part)], (1 - near) * 2 + far),
            (across.at[pl.ds(part, part)], (1 - near) * 2 + 1 - far),
        ):
            packed[pl.ds(pl.multiple_of(where * part, 16), part)] = ref[...]
    token_ref[...] = jnp.zeros_like(token_ref)
    frames, _, width, channels = held.shape
    size = count * width
    copies = []
    for f in range(frames):
        base = (5 * f) * (size // 2)
        shape = (count, width, 128)
        held[f, :, :, :128] = packed[base : base + size].reshape(shape)
        held[f, :, :, 128:256] = packed[base + size : base + 2 * size].reshape(shape)
        tails = packed[base + 2 * size : base + 2 * size + size // 2].reshape(count // 2, width, 128)
        held[f, : count // 2, :, MAIN:] = tails[:, :, :TAIL]
        held[f, count // 2 :, :, MAIN:] = tails[:, :, TAIL:]
        copies.append(move(held.at[f], out_ref.at[f, pl.ds(first, count)], sems.at[f]))
    for copy in copies:
        copy.wait()


def unpack(first, count, kind, shape, parts, token, grown):
    frames, _, width, channels = shape
    old = [] if grown is None else [grown]
    scratch = [
        pltpu.VMEM((frames, count, width, channels), BF16),
        pltpu.SemaphoreType.DMA((frames,)),
    ]
    if kind != "S":
        scratch.insert(0, pltpu.VMEM((frames * count * width * 5 // 2, 128), BF16))
    return pl.pallas_call(
        functools.partial(unpack_kernel, first, count, kind, grown is not None),
        out_shape=[jax.ShapeDtypeStruct(shape, BF16), token_spec()],
        in_specs=[hbm()] * len(old) + [vmem()] * (len(parts) + 1),
        out_specs=[hbm(), vmem()],
        scratch_shapes=scratch,
        input_output_aliases={0: 0} if old else {},
        compiler_params=pltpu.CompilerParams(vmem_limit_bytes=LIMIT),
        cost_estimate=pl.CostEstimate(
            flops=int(SCALE * (0)), bytes_accessed=int(SCALE * (4 * frames * count * width * channels)), transcendentals=0
        ),
        name=f"unpack_{first}",
    )(*old, *parts, token)


def plan(rows):
    if rows == 48:
        return [(8, 8, "A", 0), (16, 12, "B", 1), (28, 12, "A", 2), (0, 8, "B", 3), (40, 8, "A", 4)]
    size = rows // 6
    kinds = "ABABAB"
    return [(size * i, size, kinds[i], g) for g, i in enumerate((1, 2, 3, 4, 0, 5))]


def order(count):
    if count == 5:
        return [
            ("C", 0), ("T", 0), ("C", 1), ("A", 0), ("C", 2), ("L", 0),
            ("T", 1), ("C", 3), ("J", 0), ("T", 2), ("T", 3), ("A", 1),
            ("C", 4), ("A", 3), ("U", 0), ("T", 4), ("A", 2), ("L", 1),
            ("L", 2), ("L", 3), ("J", 2), ("A", 4), ("L", 4), ("J", 1),
            ("J", 3), ("J", 4), ("U", 2), ("U", 1), ("U", 4), ("U", 3),
        ]
    lags = {"C": 0, "T": 1, "A": 2, "L": 3, "J": 4, "U": 5}
    steps = []
    for slot in range(count + 6):
        for step in "CTALJU":
            chunk = slot - lags[step]
            if 0 <= chunk < count:
                steps.append((step, chunk))
    return steps


def on_device(features, offsets, conv_weight, conv_bias, time_weight, proj_weight, flags, scales):
    rows = features.shape[1]
    edge, token = edges(features, offsets)
    halo = lax.ppermute(edge, "row", [(0, 1), (1, 0)])
    chunks = plan(rows)
    windows = [(max(first - 1, 0), min(first + size + 1, rows)) for first, size, _, _ in chunks]
    early = sum(chunk[3] == 0 for chunk in chunks)
    given = (conv_weight, time_weight, proj_weight)
    *xs, main, tail, local, near, token = sums(windows[:early], features, offsets, given, token)
    weights = main, tail, local
    count = lax.axis_size("frame")
    inside = [(i, i ^ 1) for i in range(count)]
    across = [(i, i + 1) for i in range(1, count - 1, 2)]
    across += [(j, i) for i, j in across]
    blank = jnp.zeros_like(halo)
    live = [{} for _ in chunks]
    out = None
    edges_sent = ()
    swapped = {}
    for step, i in order(len(chunks)):
        first, size, kind, group = chunks[i]
        now = live[i]
        if step == "C":
            edge = halo if first == 0 or first + size == rows else blank
            now["begin"] = edges_sent[0].shape[0] if edges_sent else 0
            *edges_sent, now["part"], token = conv_rows(
                first, size, rows, xs[i], edge, weights, conv_bias, token, edges_sent
            )
            if i + 1 == len(chunks) or chunks[i + 1][3] != group:
                swapped[group] = [
                    lax.ppermute(edge, "frame", pairs) for edge, pairs in zip(edges_sent, (inside, across))
                ]
                edges_sent = ()
                if group == 0:
                    *more, token = sums(windows[early:], features, offsets, (), token, (halo,))
                    xs += more
        elif step == "T":
            send, *kept, token = terms(
                first, kind, now["begin"], *swapped[group], now["part"], near, flags, scales, token
            )
            if kind == "S":
                now["parts"] = (lax.psum(send, "branch"),)
            else:
                (now["keep"],) = kept
                now["got"] = lax.ppermute(send, "branch", ring_pairs(kind)[0])
        elif step == "A":
            half = now["keep"].shape[0] // 2
            send, now["keep"], token = small(
                f"add_{first}", functools.partial(add_kernel, kind), (half, half),
                now["keep"], now["got"], token,
            )
            now["got"] = lax.ppermute(send, "branch", ring_pairs(kind)[1])
        elif step == "L":
            now["mine"], token = small(
                f"last_{first}", add_last_kernel, now["keep"].shape[:1], now["keep"], now["got"], token
            )
            now["other"] = lax.ppermute(now["mine"], "branch", ring_pairs(kind)[1])
        elif step == "J":
            both, token = small(
                f"join_{first}", join_kernel, (2 * now["mine"].shape[0],),
                now["mine"], now["other"], token,
            )
            now["parts"] = now["mine"], now["other"], lax.ppermute(both, "branch", ring_pairs(kind)[0])
        else:
            out, token = unpack(first, size, kind, features.shape, now["parts"], token, out)
    return out


def solution(mesh):
    return jax.shard_map(
        on_device,
        mesh=mesh,
        in_specs=(
            P("frame", "row", None, None),
            P("branch", "frame", "row", None, None),
            P("branch", None, None, None, None),
            P("branch", None),
            P("branch", None, None, None),
            P("branch", None, None),
            P(None, "frame"),
            P(),
        ),
        out_specs=P("frame", "row", None, None),
        check_vma=False,
    )
```

```python
import functools

import jax
import jax.numpy as jnp
from jax import lax
from jax.experimental import pallas as pl
from jax.experimental.pallas import tpu as pltpu
from jax.sharding import PartitionSpec as P

F32 = jnp.float32
BF16 = jnp.bfloat16
PART = jnp.bfloat16
SCALE = 1.0
MAIN = 256
TAIL = 64
LIMIT = 20 * 1024 * 1024
WIDE = 45 * 1024 * 1024
MUCH = 45 * 1024 * 1024
CONV = 20 * 1024 * 1024


def vmem():
    return pl.BlockSpec(memory_space=pltpu.VMEM)


def smem():
    return pl.BlockSpec(memory_space=pltpu.SMEM)


def hbm():
    return pl.BlockSpec(memory_space=pltpu.HBM)


def token_spec():
    return jax.ShapeDtypeStruct((8, 128), F32)


def move(src, dst, sem):
    copy = pltpu.make_async_copy(src, dst, sem)
    copy.start()
    return copy


def pack_to(ref, start, value):
    size = value.shape[0]
    half = size // 2
    ref[pl.ds(start, size)] = value[:, :128]
    ref[pl.ds(start + size, size)] = value[:, 128:MAIN]
    ref[pl.ds(start + 2 * size, half)] = jnp.concatenate(
        [value[:half, MAIN:], value[half:, MAIN:]], axis=1
    )


def unpack_from(ref, start, size):
    half = size // 2
    tail = ref[pl.ds(start + 2 * size, half)]
    return (
        ref[pl.ds(start, size)],
        ref[pl.ds(start + size, size)],
        jnp.concatenate([tail[:, :TAIL], tail[:, TAIL:]], axis=0),
    )


def edge_kernel(feat_ref, off_ref, out_ref, token_ref, feat, off, sems):
    token_ref[...] = jnp.zeros_like(token_ref)
    frames, rows, width, channels = feat_ref.shape
    row = jnp.where(lax.axis_index("row") == 0, rows - 1, 0)
    copies = []
    for f in range(frames):
        copies.append(move(feat_ref.at[f, row], feat.at[f], sems.at[f, 0]))
        copies.append(move(off_ref.at[0, f, row], off.at[f], sems.at[f, 1]))
    for copy in copies:
        copy.wait()
    x = (feat[...].astype(F32) + off[...].astype(F32)).astype(BF16)
    for f in range(frames):
        pack_to(out_ref, f * width * 5 // 2, x[f])


def edges(features, offsets):
    frames, rows, width, channels = features.shape
    return pl.pallas_call(
        edge_kernel,
        out_shape=[jax.ShapeDtypeStruct((frames * width * 5 // 2, 128), BF16), token_spec()],
        in_specs=[hbm(), hbm()],
        out_specs=[vmem(), vmem()],
        scratch_shapes=[
            pltpu.VMEM((frames, width, channels), BF16),
            pltpu.VMEM((frames, width, channels), BF16),
            pltpu.SemaphoreType.DMA((frames, 2)),
        ],
        name="edges",
    )(features, offsets)


def ring_bits(kind):
    z = lax.axis_index("branch")
    u = jnp.where((z == 1) | (z == 2), 1, 0)
    v = jnp.where(z >= 2, 1, 0)
    return (u, v) if kind == "A" else (v, u)


def ring_pairs(kind):
    first = [(0, 1), (1, 0), (2, 3), (3, 2)]
    second = [(1, 2), (2, 1), (3, 0), (0, 3)]
    return (first, second) if kind == "A" else (second, first)


def weights_kernel(conv_ref, time_ref, proj_ref, main_ref, tail_ref, local_ref, near_ref,
                   conv, time, proj, sems):
    loads = [move(conv_ref.at[0], conv, sems.at[0]), move(time_ref.at[0], time, sems.at[1]),
             move(proj_ref.at[0], proj, sems.at[2])]
    loads[1].wait()
    loads[2].wait()
    last = proj[...]
    channels = last.shape[0]
    both = [jnp.dot(time[k], last, preferred_element_type=F32).astype(BF16) for k in range(3)]
    near_ref[0] = both[0]
    near_ref[1] = both[2]
    for f, blocks in enumerate(((last, both[1], both[2]), (last, both[0], both[1]))):
        for k, w in enumerate(blocks):
            local_ref[f, k * MAIN : (k + 1) * MAIN] = w[:MAIN]
            local_ref[f, 3 * MAIN + k * TAIL : 3 * MAIN + (k + 1) * TAIL] = w[MAIN:]
        local_ref[f, 3 * MAIN + 3 * TAIL :] = jnp.zeros((TAIL, channels), BF16)
    zero = jnp.zeros((TAIL, MAIN), BF16)
    loads[0].wait()
    for p in range(3):
        for q in range(3):
            w = conv[p, q]
            main_ref[p, q * MAIN : (q + 1) * MAIN] = w[:MAIN, :MAIN]
            main_ref[p, 3 * MAIN + q * TAIL : 3 * MAIN + (q + 1) * TAIL] = w[MAIN:, :MAIN]
        main_ref[p, 3 * MAIN + 3 * TAIL :] = zero
    for q in range(3):
        w = jnp.concatenate(
            [conv[p, q][:, MAIN:] for p in range(3)] + [jnp.zeros((MAIN + TAIL, TAIL), BF16)],
            axis=1,
        )
        tail_ref[q * MAIN : (q + 1) * MAIN] = w[:MAIN]
        tail_ref[3 * MAIN + q * TAIL : 3 * MAIN + (q + 1) * TAIL] = w[MAIN:]
    tail_ref[3 * MAIN + 3 * TAIL :] = zero


def sums_kernel(windows, with_weights, feat_ref, off_ref, *refs):
    count = len(windows)
    frames, rows, width, channels = feat_ref.shape
    if not with_weights:
        _, *refs = refs
    if with_weights:
        conv_ref, time_ref, proj_ref, _, *refs = refs
    else:
        _, *refs = refs
    x_refs, refs = refs[:count], refs[count:]
    if with_weights:
        made, refs = refs[:4], refs[4:]
    token_ref, feat, off, sems, *refs = refs
    token_ref[...] = jnp.zeros_like(token_ref)
    copies = []
    for i, (low, high) in enumerate(windows):
        span = high - low
        for f in range(frames):
            window, place = pl.ds(low, span), pl.ds(sum(h - l for l, h in windows[:i]), span)
            copies.append((
                x_refs[i].at[f], f, place,
                move(feat_ref.at[f, window], feat.at[f, place], sems.at[i, f, 0]),
                move(off_ref.at[0, f, window], off.at[f, place], sems.at[i, f, 1]),
            ))
    if with_weights:
        weights_kernel(conv_ref, time_ref, proj_ref, *made, *refs)
    for x_ref, f, place, one, two in copies:
        one.wait()
        two.wait()
        x_ref[...] = feat[f, place] + off[f, place]


def sums(windows, features, offsets, weights, token, early=()):
    frames, rows, width, channels = features.shape
    total = sum(high - low for low, high in windows)
    out = [jax.ShapeDtypeStruct((frames, high - low, width, channels), BF16) for low, high in windows]
    scratch = [
        pltpu.VMEM((frames, total, width, channels), BF16),
        pltpu.VMEM((frames, total, width, channels), BF16),
        pltpu.SemaphoreType.DMA((len(windows), frames, 2)),
    ]
    if weights:
        out += [
            jax.ShapeDtypeStruct((3, 4 * MAIN, MAIN), BF16),
            jax.ShapeDtypeStruct((4 * MAIN, MAIN), BF16),
            jax.ShapeDtypeStruct((2, 4 * MAIN, channels), BF16),
            jax.ShapeDtypeStruct((2, channels, channels), BF16),
        ]
        scratch += [pltpu.VMEM(w.shape[1:], BF16) for w in weights]
        scratch += [pltpu.SemaphoreType.DMA((3,))]
    out.append(token_spec())
    return pl.pallas_call(
        functools.partial(sums_kernel, tuple(windows), bool(weights)),
        out_shape=out,
        in_specs=[hbm()] * (2 + len(weights)) + [vmem()] * (1 + len(early)),
        out_specs=[vmem()] * len(out),
        scratch_shapes=scratch,
        compiler_params=pltpu.CompilerParams(vmem_limit_bytes=WIDE if weights else MUCH),
        name="sums_weights" if weights else "sums",
    )(features, offsets, *weights, *early, token)


def silu(v):
    half = 0.5 * v
    return half + half * jnp.tanh(half)


def conv_kernel(first, count, rows, x_ref, halo_ref, main_ref, tail_ref, local_ref, bias_ref, _, *rest):
    *prior, near_ref, far_ref, part_ref, token_ref, cols3, cols4, outs = rest
    token_ref[...] = jnp.zeros_like(token_ref)
    frames, _, width, channels = x_ref.shape
    begin = first - max(first - 1, 0)
    span, size = count + 2, count * width
    side = lax.axis_index("row")
    bias = bias_ref[...]
    column = lax.broadcasted_iota(jnp.int32, (span, width, 1), 1)
    for f in range(frames):
        x = x_ref[f].astype(F32)
        for here, at, outside in ((first == 0, 0, 0), (first + count == rows, 1, 1)):
            if here:
                pieces = unpack_from(halo_ref, f * width * 5 // 2, width)
                edge = jnp.concatenate(pieces, axis=1).astype(F32)
                edge = (edge * jnp.where(side == outside, 0.0, 1.0))[None]
                x = jnp.concatenate([edge, x] if at == 0 else [x, edge], axis=0)
        flat = x.reshape(span * width, channels)
        before = pltpu.roll(flat, 1, 0).reshape(x.shape)
        after = pltpu.roll(flat, span * width - 1, 0).reshape(x.shape)
        before = jnp.where(column == 0, 0.0, before).reshape(flat.shape)
        after = jnp.where(column == width - 1, 0.0, after).reshape(flat.shape)
        parts = [v.astype(BF16) for v in (before, flat, after)]
        for q in range(3):
            cols3[f, :, q * MAIN : (q + 1) * MAIN] = parts[q][:, :MAIN]
        cols3[f, :, 3 * MAIN :] = jnp.concatenate(
            [v[:, MAIN:] for v in parts] + [jnp.zeros((span * width, TAIL), BF16)], axis=1
        )
        acc = bias[:, :MAIN]
        for p in range(3):
            acc = acc + jnp.dot(
                cols3[f, p * width : p * width + size], main_ref[p], preferred_element_type=F32
            )
        main = silu(acc).astype(BF16)
        three = jnp.dot(cols3[f], tail_ref[...], preferred_element_type=F32)
        acc = bias[:, MAIN:]
        for p in range(3):
            acc = acc + three[p * width : p * width + size, p * TAIL : (p + 1) * TAIL]
        tail = silu(acc).astype(BF16)
        outs[f, :size] = main[:, :128]
        outs[f, size : 2 * size] = main[:, 128:]
        outs[f, 2 * size :] = jnp.concatenate([tail[: size // 2], tail[size // 2 :]], axis=1)
        for g in range(frames):
            cols4[g, :, (f + 1) * MAIN : (f + 2) * MAIN] = main
        cols4[f, :, :MAIN] = parts[1][width : width + size, :MAIN]
    for f in range(frames):
        tails = [x_ref[f, begin : begin + count].reshape(size, channels)[:, MAIN:]]
        tails += [unpack_from(outs.at[g], 0, size)[2] for g in range(frames)]
        tails.append(jnp.zeros((size, TAIL), BF16))
        cols4[f, :, 3 * MAIN :] = jnp.concatenate(tails, axis=1)
        total = jnp.dot(cols4[f], local_ref[f], preferred_element_type=F32)
        pack_to(part_ref, f * size * 5 // 2, total.astype(PART))
    odd = lax.rem(lax.axis_index("frame"), 2)
    for ref, which, old in zip((near_ref, far_ref), (1 - odd, odd), prior or (None, None)):
        held = 0 if old is None else old.shape[0]
        if held:
            ref[:held] = old[...]
        ref[held:] = outs[which]


def conv_rows(first, count, rows, x, halo, weights, bias, token, prior):
    frames, _, width, channels = x.shape
    span, size = count + 2, count * width
    held = prior[0].shape[0] if prior else 0
    own = jax.ShapeDtypeStruct((held + size * 5 // 2, 128), BF16)
    return pl.pallas_call(
        functools.partial(conv_kernel, first, count, rows),
        out_shape=[own, own, jax.ShapeDtypeStruct((frames * size * 5 // 2, 128), PART), token_spec()],
        in_specs=[vmem()] * (7 + len(prior)),
        out_specs=[vmem()] * 4,
        scratch_shapes=[
            pltpu.VMEM((frames, span * width, 4 * MAIN), BF16),
            pltpu.VMEM((frames, size, 4 * MAIN), BF16),
            pltpu.VMEM((frames, size * 5 // 2, 128), BF16),
        ],
        compiler_params=pltpu.CompilerParams(vmem_limit_bytes=CONV),
        cost_estimate=pl.CostEstimate(
            flops=int(SCALE * (2 * frames * size * 12 * channels * channels)),
            bytes_accessed=int(SCALE * (6 * frames * size * channels)),
            transcendentals=int(SCALE * (frames * size * channels)),
        ),
        name=f"conv_{first}",
    )(x, halo, *weights[:3], bias, token, *prior)


def term_kernel(kind, begin, inside_ref, across_ref, part_ref, near_ref, flag_ref, scale_ref, _, *rest):
    *out_refs, token_ref, packed = rest
    token_ref[...] = jnp.zeros_like(token_ref)
    size = part_ref.shape[0] // 5
    odd = lax.rem(lax.axis_index("frame"), 2)
    branch = lax.axis_index("branch")
    control = jnp.maximum(branch - 1, 0)
    target = out_refs[0] if kind == "S" else packed
    for f, ref in ((1 - odd, inside_ref), (odd, across_ref)):
        base = f * (size * 5 // 2)
        value = jnp.concatenate(unpack_from(ref, begin, size), axis=1)
        term = jnp.dot(value, near_ref[f], preferred_element_type=F32)
        gain = scale_ref[control].astype(F32) / 8.0 * flag_ref[control, f].astype(F32)
        gain = jnp.where(branch == 0, 1.0, gain)
        pieces = [
            term[:, :128],
            term[:, 128:MAIN],
            jnp.concatenate([term[: size // 2, MAIN:], term[size // 2 :, MAIN:]], axis=1),
        ]
        for piece, start in zip(pieces, (base, base + size, base + 2 * size)):
            where = pl.ds(pl.multiple_of(start, 16), piece.shape[0])
            target[where] = ((piece + part_ref[where].astype(F32)) * gain).astype(BF16)
    if kind != "S":
        near_bit, _ = ring_bits(kind)
        half = packed.shape[0] // 2
        for ref, which in zip(out_refs, (1 - near_bit, near_bit)):
            ref[...] = packed[pl.ds(pl.multiple_of(which * half, 16), half)]


def terms(name, kind, begin, prev, after, part, near, flags, scales, token):
    total = part.shape[0]
    parts = 1 if kind == "S" else 2
    return pl.pallas_call(
        functools.partial(term_kernel, kind, begin),
        out_shape=[jax.ShapeDtypeStruct((total // parts, 128), BF16)] * parts + [token_spec()],
        in_specs=[vmem()] * 4 + [smem()] * 2 + [vmem()],
        out_specs=[vmem()] * (parts + 1),
        scratch_shapes=[pltpu.VMEM((total, 128), BF16)],
        compiler_params=pltpu.CompilerParams(vmem_limit_bytes=LIMIT),
        cost_estimate=pl.CostEstimate(
            flops=int(SCALE * (2 * total * 128 * 320)), bytes_accessed=int(SCALE * (10 * total * 128)), transcendentals=0
        ),
        name=f"terms_{name}",
    )(prev, after, part, near, flags, scales, token)


def add_kernel(kind, keep_ref, got_ref, _, send_ref, next_ref, token_ref):
    token_ref[...] = jnp.zeros_like(token_ref)
    _, far = ring_bits(kind)
    half = keep_ref.shape[0] // 2
    for ref, which in zip((send_ref, next_ref), (1 - far, far)):
        part = pl.ds(pl.multiple_of(which * half, 16), half)
        ref[...] = (keep_ref[part].astype(F32) + got_ref[part].astype(F32)).astype(BF16)


def add_last_kernel(keep_ref, got_ref, _, sum_ref, token_ref):
    token_ref[...] = jnp.zeros_like(token_ref)
    sum_ref[...] = (keep_ref[...].astype(F32) + got_ref[...].astype(F32)).astype(BF16)


def join_kernel(mine_ref, other_ref, _, both_ref, token_ref):
    token_ref[...] = jnp.zeros_like(token_ref)
    size = mine_ref.shape[0]
    both_ref[:size] = mine_ref[...]
    both_ref[size:] = other_ref[...]


def small(name, kernel, shapes, *operands):
    return pl.pallas_call(
        kernel,
        out_shape=[jax.ShapeDtypeStruct((rows, 128), BF16) for rows in shapes] + [token_spec()],
        in_specs=[vmem()] * len(operands),
        out_specs=[vmem()] * (len(shapes) + 1),
        compiler_params=pltpu.CompilerParams(vmem_limit_bytes=LIMIT),
        cost_estimate=pl.CostEstimate(
            flops=int(SCALE * (shapes[0] * 128)), bytes_accessed=int(SCALE * (6 * shapes[0] * 128)), transcendentals=0
        ),
        name=name,
    )(*operands)


def unpack_kernel(first, count, kind, grown, *refs):
    if grown:
        refs = refs[1:]
    if kind == "S":
        packed, _, out_ref, token_ref, held, sems = refs
    else:
        mine, other, across, _, out_ref, token_ref, packed, held, sems = refs
        near, far = ring_bits(kind)
        part = mine.shape[0]
        for ref, where in (
            (mine, near * 2 + far),
            (other, near * 2 + 1 - far),
            (across.at[pl.ds(0, part)], (1 - near) * 2 + far),
            (across.at[pl.ds(part, part)], (1 - near) * 2 + 1 - far),
        ):
            packed[pl.ds(pl.multiple_of(where * part, 16), part)] = ref[...]
    token_ref[...] = jnp.zeros_like(token_ref)
    frames, _, width, channels = held.shape
    size = count * width
    copies = []
    for f in range(frames):
        base = (5 * f) * (size // 2)
        shape = (count, width, 128)
        held[f, :, :, :128] = packed[base : base + size].reshape(shape)
        held[f, :, :, 128:256] = packed[base + size : base + 2 * size].reshape(shape)
        tails = packed[base + 2 * size : base + 2 * size + size // 2].reshape(count // 2, width, 128)
        held[f, : count // 2, :, MAIN:] = tails[:, :, :TAIL]
        held[f, count // 2 :, :, MAIN:] = tails[:, :, TAIL:]
        copies.append(move(held.at[f], out_ref.at[f, pl.ds(first, count)], sems.at[f]))
    for copy in copies:
        copy.wait()


def unpack(first, count, kind, shape, parts, token, grown):
    frames, _, width, channels = shape
    old = [] if grown is None else [grown]
    scratch = [
        pltpu.VMEM((frames, count, width, channels), BF16),
        pltpu.SemaphoreType.DMA((frames,)),
    ]
    if kind != "S":
        scratch.insert(0, pltpu.VMEM((frames * count * width * 5 // 2, 128), BF16))
    return pl.pallas_call(
        functools.partial(unpack_kernel, first, count, kind, grown is not None),
        out_shape=[jax.ShapeDtypeStruct(shape, BF16), token_spec()],
        in_specs=[hbm()] * len(old) + [vmem()] * (len(parts) + 1),
        out_specs=[hbm(), vmem()],
        scratch_shapes=scratch,
        input_output_aliases={0: 0} if old else {},
        compiler_params=pltpu.CompilerParams(vmem_limit_bytes=LIMIT),
        cost_estimate=pl.CostEstimate(
            flops=int(SCALE * (0)), bytes_accessed=int(SCALE * (4 * frames * count * width * channels)), transcendentals=0
        ),
        name=f"unpack_{first}",
    )(*old, *parts, token)


def plan(rows):
    if rows == 48:
        return [(8, 8, "A", 0), (16, 12, "B", 1), (28, 12, "A", 2), (0, 8, "B", 3), (40, 8, "A", 4)]
    size = rows // 6
    kinds = "ABABAB"
    return [(size * i, size, kinds[i], g) for g, i in enumerate((1, 2, 3, 4, 0, 5))]


def order(count):
    if count == 5:
        return [
            ("C", 0), ("T", 0), ("C", 1), ("A", 0), ("C", 2), ("L", 0),
            ("T", 1), ("C", 3), ("J", 0), ("T", 2), ("T", 3), ("A", 1),
            ("C", 4), ("A", 3), ("T", 4), ("U", 0), ("A", 2), ("L", 1),
            ("L", 2), ("L", 3), ("J", 2), ("A", 4), ("L", 4), ("J", 1),
            ("J", 3), ("J", 4), ("U", 2), ("U", 1), ("U", 4), ("U", 3),
        ]
    lags = {"C": 0, "T": 1, "A": 2, "L": 3, "J": 4, "U": 5}
    steps = []
    for slot in range(count + 6):
        for step in "CTALJU":
            chunk = slot - lags[step]
            if 0 <= chunk < count:
                steps.append((step, chunk))
    return steps


def on_device(features, offsets, conv_weight, conv_bias, time_weight, proj_weight, flags, scales):
    rows = features.shape[1]
    edge, token = edges(features, offsets)
    halo = lax.ppermute(edge, "row", [(0, 1), (1, 0)])
    chunks = plan(rows)
    windows = [(max(first - 1, 0), min(first + size + 1, rows)) for first, size, _, _ in chunks]
    early = sum(chunk[3] == 0 for chunk in chunks)
    given = (conv_weight, time_weight, proj_weight)
    *xs, main, tail, local, near, token = sums(windows[:early], features, offsets, given, token)
    weights = main, tail, local
    count = lax.axis_size("frame")
    inside = [(i, i ^ 1) for i in range(count)]
    across = [(i, i + 1) for i in range(1, count - 1, 2)]
    across += [(j, i) for i, j in across]
    blank = jnp.zeros_like(halo)
    live = [{} for _ in chunks]
    out = None
    edges_sent = ()
    swapped = {}
    for step, i in order(len(chunks)):
        first, size, kind, group = chunks[i]
        now = live[i]
        if step == "C":
            edge = halo if first == 0 or first + size == rows else blank
            now["begin"] = edges_sent[0].shape[0] if edges_sent else 0
            *edges_sent, now["part"], token = conv_rows(
                first, size, rows, xs[i], edge, weights, conv_bias, token, edges_sent
            )
            if i + 1 == len(chunks) or chunks[i + 1][3] != group:
                swapped[group] = [
                    lax.ppermute(edge, "frame", pairs) for edge, pairs in zip(edges_sent, (inside, across))
                ]
                edges_sent = ()
                if group == 0:
                    *more, token = sums(windows[early:], features, offsets, (), token, (halo,))
                    xs += more
        elif step == "T":
            send, *kept, token = terms(
                first, kind, now["begin"], *swapped[group], now["part"], near, flags, scales, token
            )
            if kind == "S":
                now["parts"] = (lax.psum(send, "branch"),)
            else:
                (now["keep"],) = kept
                now["got"] = lax.ppermute(send, "branch", ring_pairs(kind)[0])
        elif step == "A":
            half = now["keep"].shape[0] // 2
            send, now["keep"], token = small(
                f"add_{first}", functools.partial(add_kernel, kind), (half, half),
                now["keep"], now["got"], token,
            )
            now["got"] = lax.ppermute(send, "branch", ring_pairs(kind)[1])
        elif step == "L":
            now["mine"], token = small(
                f"last_{first}", add_last_kernel, now["keep"].shape[:1], now["keep"], now["got"], token
            )
            now["other"] = lax.ppermute(now["mine"], "branch", ring_pairs(kind)[1])
        elif step == "J":
            both, token = small(
                f"join_{first}", join_kernel, (2 * now["mine"].shape[0],),
                now["mine"], now["other"], token,
            )
            now["parts"] = now["mine"], now["other"], lax.ppermute(both, "branch", ring_pairs(kind)[0])
        else:
            out, token = unpack(first, size, kind, features.shape, now["parts"], token, out)
    return out


def solution(mesh):
    return jax.shard_map(
        on_device,
        mesh=mesh,
        in_specs=(
            P("frame", "row", None, None),
            P("branch", "frame", "row", None, None),
            P("branch", None, None, None, None),
            P("branch", None),
            P("branch", None, None, None),
            P("branch", None, None),
            P(None, "frame"),
            P(),
        ),
        out_specs=P("frame", "row", None, None),
        check_vma=False,
    )
```
